256 devices in a mesh: seq: 64 (over z_hi, y, x), red: 4 (over z_lo, core).
Axes of the slice: x: 4, y: 4, z: 8 (z_hi: 4, z_lo: 2; z = z_hi * 2 + z_lo), core: 2. Of those that a mesh axis runs over, the one named last changes fastest.
Arguments:
- token_ids: int32 [8192], P('seq'), may hold values from 0 to 511
- embedding: bfloat16 [512, 4096], P(None, 'red'), may hold values from -6 to 6
- proj_weight: bfloat16 [4096, 3, 4, 256], P('red', None, None, 'seq'), may hold values from -0.09375 to 0.09375
- filters: float32 [8192, 1024], P('seq', 'red'), may hold values from -1 to 1
- cotangent: float32 [8192, 1024], P('seq', 'red'), may hold values from -6 to 6
Outputs:
- output: float32 [8192, 1024], P('seq', 'red')
- filter_grad: float32 [8192, 1024], P('seq', 'red')
- branch_grads: bfloat16 [8192, 3, 1024], P('seq', None, 'red')
- weight_grad: float32 [4096, 3, 4, 256], P('red', None, None, 'seq')
The draws below stay inside these ranges and needn't reach their ends.
All inputs are finite; a program needn't handle non-finite values.
Results may differ from the reference program's by a relative error of at most 0.0029.
Values sent between devices are 32-bit elements; how exact they have to be, the bound alone decides.
No kernel may reach another device: no remote copies, remote signals or barrier semaphores. Data moves between devices by JAX's collectives and lax.ppermute only.
A program may use at most 64 MiB of HBM per device.

```python
import math
import jax
import jax.numpy as jnp
from jax import lax

D = 4096
C = 1024
VOCAB = 512
TOKENS = 8192
N_RED = 4


def draw_filters(key, part):
    rate_key, pick_key, noise_key, fast_key = jax.random.split(key, 4)
    positions = jnp.arange(TOKENS, dtype=jnp.float32)[:, None]
    slow_rates = jnp.exp(jax.random.uniform(rate_key, (C,), jnp.float32, math.log(0.1 / TOKENS), math.log(2.3 / TOKENS)))
    fast_rates = jnp.exp(jax.random.uniform(fast_key, (C,), jnp.float32, math.log(2.3 / TOKENS), math.log(1.0 / 30.0)))
    picked = jax.random.uniform(pick_key, (C,), jnp.float32)
    keeping = picked < 0.5
    noise = jnp.clip(jax.random.normal(noise_key, (TOKENS, C), jnp.float32), -4.0, 4.0)
    rates = jnp.where(keeping, slow_rates, fast_rates)
    shaped = noise * jnp.exp(-positions * rates[None, :])
    return shaped * jax.lax.rsqrt(jnp.sum(shaped * shaped, axis=0, keepdims=True))


def touch_ends(array, stream_key, least, largest):
    index_at = [jax.random.randint(jax.random.fold_in(stream_key, axis), (), 0, length) for axis, length in enumerate(array.shape)]
    main_axis = array.shape.index(max(array.shape))
    beside = index_at[:main_axis] + [(index_at[main_axis] + 1) % array.shape[main_axis]] + index_at[main_axis + 1:]
    return array.at[tuple(index_at)].set(least).at[tuple(beside)].set(largest)


def steps_of(rng, shape, shards, low, largest):
    level, own = 1.0, jax.random.fold_in(rng, 6)
    for axis_at, blocks in shards:
        steps = jnp.exp(jax.random.uniform(jax.random.fold_in(own, axis_at), (blocks,), jnp.float32, low / len(shards), largest / len(shards)))
        level = level * jnp.repeat(steps, shape[axis_at] // blocks).reshape([-1 if axis == axis_at else 1 for axis in range(len(shape))])
    return level


def scatter_about(rng, dims, width, most, shards=(), kind=jnp.bfloat16):
    array = jax.random.normal(rng, dims, jnp.float32) * width
    if len(shards) > 0:
        array = steps_of(rng, dims, shards, -0.22, 0.18) * array
    return jnp.clip(array, min=-most, max=most).astype(kind)


def setup_inputs(seed: int = 0) -> dict:
    arg_keys = jax.random.split(jax.random.key(seed), 6)
    return {
        "token_ids": touch_ends(jax.random.randint(arg_keys[0], (TOKENS,), 0, VOCAB), jax.random.fold_in(arg_keys[0], 1), 0, VOCAB - 1).astype(jnp.int32),
        "embedding": scatter_about(arg_keys[1], (VOCAB, D), 1.0, 6.0, ((1, 4),)),
        "proj_weight": scatter_about(arg_keys[2], (D, 3, N_RED, C // N_RED), D ** -0.5, 0.09375, ((0, 4), (3, 64))),
        "filters": draw_filters(jax.random.fold_in(arg_keys[5], 71), 0),
        "cotangent": scatter_about(arg_keys[4], (TOKENS, C), 1.0, 6.0, ((0, 64), (1, 4)), jnp.float32),
    }


def reference(token_ids, embedding, proj_weight, filters, cotangent):
    weight_matrix = proj_weight.reshape(D, 3 * C)
    lookup = jnp.dot(embedding, weight_matrix, preferred_element_type=jnp.float32)
    projected = jnp.take(lookup, token_ids, axis=0)
    queries = projected[:, :C]
    key_rows = projected[:, C:2 * C]
    value_rows = projected[:, 2 * C:]
    inner = key_rows * value_rows
    upstream = cotangent * queries
    length = token_ids.shape[0]
    padded = 2 * length
    spectra = jnp.fft.rfft(jnp.concatenate([filters, inner, upstream], axis=1), n=padded, axis=0)
    filt_spec = spectra[:, :C]
    inner_spec = spectra[:, C:2 * C]
    up_spec = spectra[:, 2 * C:]
    joined = jnp.concatenate([filt_spec * inner_spec, jnp.conj(filt_spec) * up_spec, up_spec * jnp.conj(inner_spec)], axis=1)
    back = jnp.fft.irfft(joined, n=padded, axis=0)[:length]
    conv = back[:, :C]
    grad_inner = back[:, C:2 * C]
    filter_raw = back[:, 2 * C:]
    scale_factor = float(TOKENS) ** -0.5
    output = queries * conv
    filter_grad = filter_raw * scale_factor
    branch_grads = jnp.stack([cotangent * conv, grad_inner * value_rows, grad_inner * key_rows], axis=1).astype(jnp.bfloat16)
    summed = jax.ops.segment_sum(branch_grads.reshape(length, 3 * C).astype(jnp.float32), token_ids, num_segments=VOCAB)
    weight_grad = jnp.dot(embedding.astype(jnp.float32).T, summed, precision=lax.Precision.HIGHEST) * scale_factor
    return output, filter_grad, branch_grads, weight_grad.reshape(D, 3, N_RED, C // N_RED)
```

```python
import functools
import math

import jax
import jax.numpy as jnp
import ml_dtypes
import numpy as np
from jax import lax
from jax.experimental import pallas as pl
from jax.experimental.pallas import tpu as pltpu
from jax.sharding import PartitionSpec as P


BLOCKS = 64
LANES = 128
OWN = 4
IN_ROWS = 9
OUT_ROWS = 20
F32 = jnp.float32
BF16 = jnp.bfloat16


def halves(matrix):
    matrix = np.asarray(matrix, np.float32)
    high = matrix.astype(ml_dtypes.bfloat16)
    low = (matrix - high.astype(np.float32)).astype(ml_dtypes.bfloat16)
    return high, low


@functools.cache
def transform_constants():
    odd = np.arange(BLOCKS) + 0.5
    theta = 2.0 * math.pi * np.outer(odd, np.arange(BLOCKS)) / LANES
    rows = np.concatenate([np.cos(theta), -np.sin(theta)], axis=0)
    high, low = halves(rows)
    first = np.concatenate([high, high, low], axis=1)
    high, low = halves(rows.T * (2.0 / (2 * BLOCKS * LANES)))
    last = np.concatenate([high, high, low], axis=1)
    phi = 2.0 * math.pi * np.outer(odd, np.arange(LANES)) / (2 * BLOCKS * LANES)
    twiddle = np.stack([np.cos(phi), np.sin(phi)]).astype(np.float32)
    psi = 2.0 * math.pi * (np.outer(np.arange(LANES), np.arange(LANES)) % LANES) / LANES
    right = np.block([[np.cos(psi), -np.sin(psi)], [np.sin(psi), np.cos(psi)]])
    forward = np.stack(halves(right))
    backward = np.stack(halves(right.T))
    return first, last, twiddle, forward, backward


def split(value):
    high = value.astype(BF16)
    return high, (value - high.astype(F32)).astype(BF16)


def dot(left, right):
    return jnp.dot(left, right, preferred_element_type=F32)


def dot_last(left, right):
    return lax.dot_general(left, right, (((1,), (1,)), ((), ())), preferred_element_type=F32)


def pack_kernel(ids_ref, filt_ref, cot_ref, out_ref, turn_ref):
    for number, ref in enumerate((filt_ref, cot_ref)):
        turn_ref[...] = ref[...].T
        for c in range(OWN):
            out_ref[pl.ds(number * OWN + c, BLOCKS, stride=IN_ROWS), :] = turn_ref[
                pl.ds(c, BLOCKS, stride=OWN), :
            ]
    out_ref[pl.ds(2 * OWN, BLOCKS, stride=IN_ROWS), :] = jnp.broadcast_to(
        ids_ref[...].astype(F32), (BLOCKS, LANES)
    )


def table_kernel(proj_ref, emb_ref, out_ref, rows_ref):
    branches, reds, piece, _ = proj_ref.shape
    wide = branches * piece
    for q in range(reds):
        for b in range(branches):
            at = q * wide + b * piece
            rows_ref[at : at + piece, :] = proj_ref[b, q].astype(F32)
    table = dot_last(rows_ref[...].astype(BF16), emb_ref[...])
    for q in range(reds):
        for part in range(table.shape[1] // LANES):
            out_ref[q, part * wide : (part + 1) * wide, :] = table[
                q * wide : (q + 1) * wide, part * LANES : (part + 1) * LANES
            ]


def right_product(value, matrix_ref):
    high, low = split(value)
    count = value.shape[0]
    both = dot(jnp.concatenate([high, low], axis=0), matrix_ref[0])
    return both[:count] + both[count:] + dot(high, matrix_ref[1])


def conv_kernel(
    scale, in_ref, parts_ref, first_ref, last_ref, twiddle_ref, forward_ref, backward_ref, out_ref, grads_ref
):
    reds, table_rows, _ = parts_ref.shape
    wide = 3 * OWN
    groups = table_rows // wide

    def received(row):
        return in_ref[pl.ds(row, BLOCKS, stride=IN_ROWS), :]

    table = parts_ref[0]
    for q in range(1, reds):
        table = table + parts_ref[q]
    ids = received(2 * OWN).astype(jnp.int32)
    lane = ids & (LANES - 1)
    group = ids >> 7

    def looked_up(column):
        value = None
        for g in range(groups):
            row = jnp.broadcast_to(table[g * wide + column : g * wide + column + 1, :], (BLOCKS, LANES))
            found = jnp.take_along_axis(row, lane, axis=1, mode="promise_in_bounds")
            value = found if value is None else jnp.where(group == g, found, value)
        return value

    queries = [looked_up(c) for c in range(OWN)]
    keys = [looked_up(OWN + c) for c in range(OWN)]
    values = [looked_up(2 * OWN + c) for c in range(OWN)]
    cotangent = [received(OWN + c) for c in range(OWN)]
    signals = [received(c) for c in range(OWN)]
    signals += [keys[c] * values[c] for c in range(OWN)]
    signals += [cotangent[c] * queries[c] for c in range(OWN)]
    count = len(signals)

    cosine, sine = twiddle_ref[0], twiddle_ref[1]
    high, low = split(jnp.concatenate(signals, axis=1))
    mixed = dot(first_ref[...], jnp.concatenate([high, low, high], axis=0))
    rows = []
    for n in range(count):
        re = mixed[:BLOCKS, n * LANES : (n + 1) * LANES]
        im = mixed[BLOCKS:, n * LANES : (n + 1) * LANES]
        rows.append(jnp.concatenate([re * cosine + im * sine, im * cosine - re * sine], axis=1))
    spectra = right_product(jnp.concatenate(rows, axis=0), forward_ref)

    def spectrum(n):
        own = spectra[n * BLOCKS : (n + 1) * BLOCKS]
        return own[:, :LANES], own[:, LANES:]

    joined = [None] * count
    for c in range(OWN):
        f_re, f_im = spectrum(c)
        i_re, i_im = spectrum(OWN + c)
        u_re, u_im = spectrum(2 * OWN + c)
        joined[c] = (f_re * i_re - f_im * i_im, f_re * i_im + f_im * i_re)
        joined[OWN + c] = (f_re * u_re + f_im * u_im, f_re * u_im - f_im * u_re)
        joined[2 * OWN + c] = (u_re * i_re + u_im * i_im, u_im * i_re - u_re * i_im)
    back = right_product(
        jnp.concatenate([jnp.concatenate(pair, axis=1) for pair in joined], axis=0), backward_ref
    )
    columns = []
    for n in range(count):
        re = back[n * BLOCKS : (n + 1) * BLOCKS, :LANES]
        im = back[n * BLOCKS : (n + 1) * BLOCKS, LANES:]
        columns.append(jnp.concatenate([re * cosine - im * sine, re * sine + im * cosine], axis=0))
    high, low = split(jnp.concatenate(columns, axis=1))
    result = dot(last_ref[...], jnp.concatenate([high, low, high], axis=0))

    grads_ref[...] = jnp.zeros_like(grads_ref)
    for c in range(OWN):
        conv = result[:, c * LANES : (c + 1) * LANES]
        grad_inner = result[:, (OWN + c) * LANES : (OWN + c + 1) * LANES]
        filter_grad = result[:, (2 * OWN + c) * LANES : (2 * OWN + c + 1) * LANES]
        grads = (cotangent[c] * conv, grad_inner * values[c], grad_inner * keys[c])
        sent = (*grads, queries[c] * conv, filter_grad * scale)
        for number, value in enumerate(sent):
            out_ref[pl.ds(number * OWN + c, BLOCKS, stride=OUT_ROWS), :] = value
        for number, value in enumerate(grads):
            grads_ref[pl.ds(number * OWN + c, BLOCKS, stride=16), :] = value


def sums_kernel(in_ref, grads_ref, out_ref, ids_ref):
    ids_ref[...] = in_ref[pl.ds(2 * OWN, BLOCKS, stride=IN_ROWS), :].astype(jnp.int32)
    groups = out_ref.shape[0] // 16
    total = jnp.zeros(out_ref.shape, F32)
    for pair in range(BLOCKS // 2):
        picked, hot = [], []
        for s in (2 * pair, 2 * pair + 1):
            ids = ids_ref[s : s + 1, :]
            grads = grads_ref[s * 16 : (s + 1) * 16, :]
            group = jnp.broadcast_to(ids >> 7, (16, LANES))
            picked.append(
                jnp.concatenate([jnp.where(group == g, grads, 0.0) for g in range(groups)], axis=0).astype(BF16)
            )
            lane = jnp.broadcast_to(ids & (LANES - 1), (LANES, LANES))
            rows = lax.broadcasted_iota(jnp.int32, (LANES, LANES), 0)
            hot.append(jnp.where(rows == lane, 1.0, 0.0).astype(BF16))
        total = total + dot_last(jnp.concatenate(picked, axis=1), jnp.concatenate(hot, axis=1))
    out_ref[...] = total


def weight_kernel(scale, sums_ref, emb_ref, out_ref):
    branches, reds, piece, _ = out_ref.shape
    groups = sums_ref.shape[1] // 16
    rows = jnp.concatenate(
        [
            jnp.concatenate([sums_ref[q, g * 16 : (g + 1) * 16, :] for g in range(groups)], axis=1)
            for q in range(reds)
        ],
        axis=0,
    )
    high, low = split(rows)
    count = rows.shape[0]
    both = dot(jnp.concatenate([high, low], axis=0), emb_ref[...])
    grad = (both[:count] + both[count:]) * scale
    for q in range(reds):
        for b in range(branches):
            at = q * 16 + b * piece
            out_ref[b, q] = grad[at : at + piece, :]


def unpack_kernel(in_ref, output_ref, filter_ref, branch_ref, turn_ref):
    for number in range(OUT_ROWS // OWN):
        for c in range(OWN):
            turn_ref[number, pl.ds(c, BLOCKS, stride=OWN), :] = in_ref[
                pl.ds(number * OWN + c, BLOCKS, stride=OUT_ROWS), :
            ]
        value = turn_ref[number].T
        if number < 3:
            branch_ref[number] = value.astype(BF16)
        elif number == 3:
            output_ref[...] = value
        else:
            filter_ref[...] = value


def call(body, outs, scratch, *operands):
    single = not isinstance(outs, (list, tuple))
    return pl.pallas_call(
        body,
        out_shape=outs if single else tuple(outs),
        scratch_shapes=scratch,
        compiler_params=pltpu.CompilerParams(vmem_limit_bytes=48 * 2**20),
    )(*operands)


def shape(dims, dtype=F32):
    return jax.ShapeDtypeStruct(dims, dtype)


def exchange(value, axis, pieces, rows):
    sent = value.reshape(pieces, 1, rows * LANES)
    got = lax.all_to_all(sent, axis, split_axis=0, concat_axis=0, tiled=True)
    return got.reshape(pieces * rows, LANES)


def shards(token_ids, embedding, proj_weight, filters, cotangent):
    reds = lax.axis_size("red")
    blocks = lax.axis_size("seq")
    width_rows, branches, _, piece = proj_weight.shape
    vocabulary = embedding.shape[0]
    groups = vocabulary // LANES
    positions, channels = filters.shape
    scale = float(positions * blocks) ** (-0.5)

    packed = call(
        pack_kernel,
        shape((BLOCKS * IN_ROWS, LANES)),
        [pltpu.VMEM((channels, LANES), F32)],
        token_ids.reshape(1, positions),
        filters,
        cotangent,
    )
    arrived = exchange(packed, "seq", BLOCKS, IN_ROWS)
    table = call(
        table_kernel,
        shape((reds, groups * branches * piece, LANES)),
        [pltpu.VMEM((reds * branches * piece, width_rows), F32)],
        proj_weight.transpose(1, 2, 3, 0),
        embedding,
    )
    parts = lax.all_to_all(table, "red", split_axis=0, concat_axis=0, tiled=True)
    constants = [jnp.asarray(c) for c in transform_constants()]
    results, grads = call(
        functools.partial(conv_kernel, scale),
        [shape((BLOCKS * OUT_ROWS, LANES)), shape((BLOCKS * 16, LANES))],
        [],
        arrived,
        parts,
        *constants,
    )
    returned = exchange(results, "seq", BLOCKS, OUT_ROWS)
    sums = call(
        sums_kernel,
        shape((groups * 16, LANES)),
        [pltpu.VMEM((BLOCKS, LANES), jnp.int32)],
        arrived,
        grads,
    )
    gathered = lax.all_gather(sums, "red", axis=0)
    weight_grad = call(
        functools.partial(weight_kernel, scale),
        shape((branches, reds, piece, width_rows)),
        [],
        gathered,
        embedding,
    )
    output, filter_grad, branch_grads = call(
        unpack_kernel,
        [
            shape((positions, channels)),
            shape((positions, channels)),
            shape((branches, positions, channels), BF16),
        ],
        [pltpu.VMEM((OUT_ROWS // OWN, channels, LANES), F32)],
        returned,
    )
    return output, filter_grad, branch_grads.transpose(1, 0, 2), weight_grad.transpose(3, 0, 1, 2)


def solution(mesh):
    in_specs = (
        P("seq"),
        P(None, "red"),
        P("red", None, None, "seq"),
        P("seq", "red"),
        P("seq", "red"),
    )
    out_specs = (
        P("seq", "red"),
        P("seq", "red"),
        P("seq", None, "red"),
        P("red", None, None, "seq"),
    )
    return jax.shard_map(shards, mesh=mesh, in_specs=in_specs, out_specs=out_specs, check_vma=False)
```

```python
import functools
import math

import jax
import jax.numpy as jnp
import ml_dtypes
import numpy as np
from jax import lax
from jax.experimental import pallas as pl
from jax.experimental.pallas import tpu as pltpu
from jax.sharding import PartitionSpec as P


BLOCKS = 64
LANES = 128
OWN = 4
IN_ROWS = 9
OUT_ROWS = 20
F32 = jnp.float32
BF16 = jnp.bfloat16


def halves(matrix):
    matrix = np.asarray(matrix, np.float32)
    high = matrix.astype(ml_dtypes.bfloat16)
    low = (matrix - high.astype(np.float32)).astype(ml_dtypes.bfloat16)
    return high, low


@functools.cache
def transform_constants():
    odd = np.arange(BLOCKS) + 0.5
    theta = 2.0 * math.pi * np.outer(odd, np.arange(BLOCKS)) / LANES
    rows = np.concatenate([np.cos(theta), -np.sin(theta)], axis=0)
    high, low = halves(rows)
    first = np.concatenate([high, high, low], axis=1)
    high, low = halves(rows.T * (2.0 / (2 * BLOCKS * LANES)))
    last = np.concatenate([high, high, low], axis=1)
    phi = 2.0 * math.pi * np.outer(odd, np.arange(LANES)) / (2 * BLOCKS * LANES)
    twiddle = np.stack([np.cos(phi), np.sin(phi)]).astype(np.float32)
    psi = 2.0 * math.pi * (np.outer(np.arange(LANES), np.arange(LANES)) % LANES) / LANES
    right = np.block([[np.cos(psi), -np.sin(psi)], [np.sin(psi), np.cos(psi)]])
    forward = np.stack(halves(right))
    backward = np.stack(halves(right.T))
    return first, last, twiddle, forward, backward


def split(value):
    high = value.astype(BF16)
    return high, (value - high.astype(F32)).astype(BF16)


def dot(left, right):
    return jnp.dot(left, right, preferred_element_type=F32)


def dot_last(left, right):
    return lax.dot_general(left, right, (((1,), (1,)), ((), ())), preferred_element_type=F32)


def pack_kernel(ids_ref, filt_ref, cot_ref, out_ref, turn_ref):
    for number, ref in enumerate((filt_ref, cot_ref)):
        turn_ref[...] = ref[...].T
        for c in range(OWN):
            out_ref[pl.ds(number * OWN + c, BLOCKS, stride=IN_ROWS), :] = turn_ref[
                pl.ds(c, BLOCKS, stride=OWN), :
            ]
    out_ref[pl.ds(2 * OWN, BLOCKS, stride=IN_ROWS), :] = jnp.broadcast_to(
        ids_ref[...].astype(F32), (BLOCKS, LANES)
    )


def table_kernel(proj_ref, emb_ref, out_ref, rows_ref):
    branches, reds, piece, _ = proj_ref.shape
    wide = branches * piece
    for q in range(reds):
        for b in range(branches):
            at = q * wide + b * piece
            rows_ref[at : at + piece, :] = proj_ref[b, q].astype(F32)
    table = dot_last(rows_ref[...].astype(BF16), emb_ref[...])
    for q in range(reds):
        for part in range(table.shape[1] // LANES):
            at = q * table.shape[1] // LANES * wide + part * wide
            out_ref[at : at + wide, :] = table[
                q * wide : (q + 1) * wide, part * LANES : (part + 1) * LANES
            ]


def right_product(value, matrix_ref):
    high, low = split(value)
    count = value.shape[0]
    both = dot(jnp.concatenate([high, low], axis=0), matrix_ref[0])
    return both[:count] + both[count:] + dot(high, matrix_ref[1])


def conv_kernel(
    scale, place_ref, in_ref, parts_ref, first_ref, last_ref, twiddle_ref, forward_ref, backward_ref, out_ref, grads_ref
):
    reds = parts_ref.shape[0]
    table_rows = parts_ref.shape[1] // reds
    wide = 3 * OWN
    groups = table_rows // wide
    own_rows = pl.ds(pl.multiple_of(place_ref[0] * table_rows, 8), table_rows)

    def received(row):
        return in_ref[pl.ds(row, BLOCKS, stride=IN_ROWS), :]

    table = parts_ref[0, own_rows, :]
    for q in range(1, reds):
        table = table + parts_ref[q, own_rows, :]
    ids = received(2 * OWN).astype(jnp.int32)
    lane = ids & (LANES - 1)
    group = ids >> 7

    def looked_up(column):
        value = None
        for g in range(groups):
            row = jnp.broadcast_to(table[g * wide + column : g * wide + column + 1, :], (BLOCKS, LANES))
            found = jnp.take_along_axis(row, lane, axis=1, mode="promise_in_bounds")
            value = found if value is None else jnp.where(group == g, found, value)
        return value

    queries = [looked_up(c) for c in range(OWN)]
    keys = [looked_up(OWN + c) for c in range(OWN)]
    values = [looked_up(2 * OWN + c) for c in range(OWN)]
    cotangent = [received(OWN + c) for c in range(OWN)]
    signals = [received(c) for c in range(OWN)]
    signals += [keys[c] * values[c] for c in range(OWN)]
    signals += [cotangent[c] * queries[c] for c in range(OWN)]
    count = len(signals)

    cosine, sine = twiddle_ref[0], twiddle_ref[1]
    high, low = split(jnp.concatenate(signals, axis=1))
    mixed = dot(first_ref[...], jnp.concatenate([high, low, high], axis=0))
    rows = []
    for n in range(count):
        re = mixed[:BLOCKS, n * LANES : (n + 1) * LANES]
        im = mixed[BLOCKS:, n * LANES : (n + 1) * LANES]
        rows.append(jnp.concatenate([re * cosine + im * sine, im * cosine - re * sine], axis=1))
    spectra = right_product(jnp.concatenate(rows, axis=0), forward_ref)

    def spectrum(n):
        own = spectra[n * BLOCKS : (n + 1) * BLOCKS]
        return own[:, :LANES], own[:, LANES:]

    joined = [None] * count
    for c in range(OWN):
        f_re, f_im = spectrum(c)
        i_re, i_im = spectrum(OWN + c)
        u_re, u_im = spectrum(2 * OWN + c)
        joined[c] = (f_re * i_re - f_im * i_im, f_re * i_im + f_im * i_re)
        joined[OWN + c] = (f_re * u_re + f_im * u_im, f_re * u_im - f_im * u_re)
        joined[2 * OWN + c] = (u_re * i_re + u_im * i_im, u_im * i_re - u_re * i_im)
    back = right_product(
        jnp.concatenate([jnp.concatenate(pair, axis=1) for pair in joined], axis=0), backward_ref
    )
    columns = []
    for n in range(count):
        re = back[n * BLOCKS : (n + 1) * BLOCKS, :LANES]
        im = back[n * BLOCKS : (n + 1) * BLOCKS, LANES:]
        columns.append(jnp.concatenate([re * cosine - im * sine, re * sine + im * cosine], axis=0))
    high, low = split(jnp.concatenate(columns, axis=1))
    result = dot(last_ref[...], jnp.concatenate([high, low, high], axis=0))

    grads_ref[...] = jnp.zeros_like(grads_ref)
    for c in range(OWN):
        conv = result[:, c * LANES : (c + 1) * LANES]
        grad_inner = result[:, (OWN + c) * LANES : (OWN + c + 1) * LANES]
        filter_grad = result[:, (2 * OWN + c) * LANES : (2 * OWN + c + 1) * LANES]
        grads = (cotangent[c] * conv, grad_inner * values[c], grad_inner * keys[c])
        sent = (*grads, queries[c] * conv, filter_grad * scale)
        for number, value in enumerate(sent):
            out_ref[pl.ds(number * OWN + c, BLOCKS, stride=OUT_ROWS), :] = value
        for number, value in enumerate(grads):
            grads_ref[pl.ds(number * OWN + c, BLOCKS, stride=16), :] = value


def sums_kernel(in_ref, grads_ref, out_ref, ids_ref):
    ids_ref[...] = in_ref[pl.ds(2 * OWN, BLOCKS, stride=IN_ROWS), :].astype(jnp.int32)
    groups = out_ref.shape[0] // 16
    total = jnp.zeros(out_ref.shape, F32)
    for pair in range(BLOCKS // 2):
        picked, hot = [], []
        for s in (2 * pair, 2 * pair + 1):
            ids = ids_ref[s : s + 1, :]
            grads = grads_ref[s * 16 : (s + 1) * 16, :]
            group = jnp.broadcast_to(ids >> 7, (16, LANES))
            picked.append(
                jnp.concatenate([jnp.where(group == g, grads, 0.0) for g in range(groups)], axis=0).astype(BF16)
            )
            lane = jnp.broadcast_to(ids & (LANES - 1), (LANES, LANES))
            rows = lax.broadcasted_iota(jnp.int32, (LANES, LANES), 0)
            hot.append(jnp.where(rows == lane, 1.0, 0.0).astype(BF16))
        total = total + dot_last(jnp.concatenate(picked, axis=1), jnp.concatenate(hot, axis=1))
    out_ref[...] = total


def weight_kernel(scale, sums_ref, emb_ref, out_ref):
    branches, reds, piece, _ = out_ref.shape
    groups = sums_ref.shape[1] // 16
    rows = jnp.concatenate(
        [
            jnp.concatenate([sums_ref[q, g * 16 : (g + 1) * 16, :] for g in range(groups)], axis=1)
            for q in range(reds)
        ],
        axis=0,
    )
    high, low = split(rows)
    count = rows.shape[0]
    both = dot(jnp.concatenate([high, low], axis=0), emb_ref[...])
    grad = (both[:count] + both[count:]) * scale
    for q in range(reds):
        for b in range(branches):
            at = q * 16 + b * piece
            out_ref[b, q] = grad[at : at + piece, :]


def unpack_kernel(in_ref, output_ref, filter_ref, branch_ref, turn_ref):
    for number in range(OUT_ROWS // OWN):
        for c in range(OWN):
            turn_ref[number, pl.ds(c, BLOCKS, stride=OWN), :] = in_ref[
                pl.ds(number * OWN + c, BLOCKS, stride=OUT_ROWS), :
            ]
        value = turn_ref[number].T
        if number < 3:
            branch_ref[number] = value.astype(BF16)
        elif number == 3:
            output_ref[...] = value
        else:
            filter_ref[...] = value


def call(body, outs, scratch, *operands, scalars=0):
    single = not isinstance(outs, (list, tuple))
    spaces = [pltpu.SMEM] * scalars + [pltpu.VMEM] * (len(operands) - scalars)
    return pl.pallas_call(
        body,
        in_specs=[pl.BlockSpec(memory_space=space) for space in spaces],
        out_shape=outs if single else tuple(outs),
        scratch_shapes=scratch,
        compiler_params=pltpu.CompilerParams(vmem_limit_bytes=48 * 2**20),
    )(*operands)


def shape(dims, dtype=F32):
    return jax.ShapeDtypeStruct(dims, dtype)


def exchange(value, axis, pieces, rows):
    sent = value.reshape(pieces, 1, rows * LANES)
    got = lax.all_to_all(sent, axis, split_axis=0, concat_axis=0, tiled=True)
    return got.reshape(pieces * rows, LANES)


def shards(token_ids, embedding, proj_weight, filters, cotangent):
    reds = lax.axis_size("red")
    blocks = lax.axis_size("seq")
    width_rows, branches, _, piece = proj_weight.shape
    vocabulary = embedding.shape[0]
    groups = vocabulary // LANES
    positions, channels = filters.shape
    scale = float(positions * blocks) ** (-0.5)

    packed = call(
        pack_kernel,
        shape((BLOCKS * IN_ROWS, LANES)),
        [pltpu.VMEM((channels, LANES), F32)],
        token_ids.reshape(1, positions),
        filters,
        cotangent,
    )
    arrived = exchange(packed, "seq", BLOCKS, IN_ROWS)
    table = call(
        table_kernel,
        shape((reds * groups * branches * piece, LANES)),
        [pltpu.VMEM((reds * branches * piece, width_rows), F32)],
        proj_weight.transpose(1, 2, 3, 0),
        embedding,
    )
    parts = lax.all_gather(table, "red", axis=0)
    constants = [jnp.asarray(c) for c in transform_constants()]
    results, grads = call(
        functools.partial(conv_kernel, scale),
        [shape((BLOCKS * OUT_ROWS, LANES)), shape((BLOCKS * 16, LANES))],
        [],
        lax.axis_index("red").reshape(1),
        arrived,
        parts,
        *constants,
        scalars=1,
    )
    returned = exchange(results, "seq", BLOCKS, OUT_ROWS)
    sums = call(
        sums_kernel,
        shape((groups * 16, LANES)),
        [pltpu.VMEM((BLOCKS, LANES), jnp.int32)],
        arrived,
        grads,
    )
    gathered = lax.all_gather(sums, "red", axis=0)
    weight_grad = call(
        functools.partial(weight_kernel, scale),
        shape((branches, reds, piece, width_rows)),
        [],
        gathered,
        embedding,
    )
    output, filter_grad, branch_grads = call(
        unpack_kernel,
        [
            shape((positions, channels)),
            shape((positions, channels)),
            shape((branches, positions, channels), BF16),
        ],
        [pltpu.VMEM((OUT_ROWS // OWN, channels, LANES), F32)],
        returned,
    )
    return output, filter_grad, branch_grads.transpose(1, 0, 2), weight_grad.transpose(3, 0, 1, 2)


def solution(mesh):
    in_specs = (
        P("seq"),
        P(None, "red"),
        P("red", None, None, "seq"),
        P("seq", "red"),
        P("seq", "red"),
    )
    out_specs = (
        P("seq", "red"),
        P("seq", "red"),
        P("seq", None, "red"),
        P("red", None, None, "seq"),
    )
    return jax.shard_map(shards, mesh=mesh, in_specs=in_specs, out_specs=out_specs, check_vma=False)
```

```python
import functools
import math

import jax
import jax.numpy as jnp
import ml_dtypes
import numpy as np
from jax import lax
from jax.experimental import pallas as pl
from jax.experimental.pallas import tpu as pltpu
from jax.sharding import PartitionSpec as P


BLOCKS = 64
LANES = 128
OWN = 4
IN_ROWS = 9
OUT_ROWS = 20
F32 = jnp.float32
BF16 = jnp.bfloat16


def halves(matrix):
    matrix = np.asarray(matrix, np.float32)
    high = matrix.astype(ml_dtypes.bfloat16)
    low = (matrix - high.astype(np.float32)).astype(ml_dtypes.bfloat16)
    return high, low


@functools.cache
def transform_constants():
    odd = np.arange(BLOCKS) + 0.5
    theta = 2.0 * math.pi * np.outer(odd, np.arange(BLOCKS)) / LANES
    rows = np.concatenate([np.cos(theta), -np.sin(theta)], axis=0)
    high, low = halves(rows)
    first = np.concatenate([high, high, low], axis=1)
    high, low = halves(rows.T * (2.0 / (2 * BLOCKS * LANES)))
    last = np.concatenate([high, high, low], axis=1)
    phi = 2.0 * math.pi * np.outer(odd, np.arange(LANES)) / (2 * BLOCKS * LANES)
    twiddle = np.stack([np.cos(phi), np.sin(phi)]).astype(np.float32)
    psi = 2.0 * math.pi * (np.outer(np.arange(LANES), np.arange(LANES)) % LANES) / LANES
    right = np.block([[np.cos(psi), -np.sin(psi)], [np.sin(psi), np.cos(psi)]])
    forward = np.stack(halves(right))
    backward = np.stack(halves(right.T))
    return first, last, twiddle, forward, backward


def split(value):
    high = value.astype(BF16)
    return high, (value - high.astype(F32)).astype(BF16)


def dot(left, right):
    return jnp.dot(left, right, preferred_element_type=F32)


def dot_last(left, right):
    return lax.dot_general(left, right, (((1,), (1,)), ((), ())), preferred_element_type=F32)


def pack_kernel(filt_hbm, cot_hbm, ids_hbm, out_ref, filt, cot, ids, turn_ref, sems):
    pairs = ((filt_hbm, filt), (cot_hbm, cot), (ids_hbm, ids))
    copies = [pltpu.make_async_copy(source, kept, sems.at[n]) for n, (source, kept) in enumerate(pairs)]
    for copy in copies:
        copy.start()
    for number, ref in enumerate((filt, cot)):
        copies[number].wait()
        turn_ref[...] = ref[...].T
        for c in range(OWN):
            out_ref[pl.ds(number * OWN + c, BLOCKS, stride=IN_ROWS), :] = turn_ref[
                pl.ds(c, BLOCKS, stride=OWN), :
            ]
    copies[2].wait()
    out_ref[pl.ds(2 * OWN, BLOCKS, stride=IN_ROWS), :] = jnp.broadcast_to(ids[...].astype(F32), (BLOCKS, LANES))


def table_kernel(proj_ref, emb_ref, *refs):
    *out_refs, rows_ref, table_ref = refs
    branches, reds, piece, _ = proj_ref.shape
    wide = branches * piece
    rows_ref[...] = jnp.zeros_like(rows_ref)
    for q in range(reds):
        for b in range(branches):
            at = q * 16 + b * piece
            rows_ref[at : at + piece, :] = proj_ref[b, q].astype(F32)
    table_ref[...] = dot_last(rows_ref[...].astype(BF16), emb_ref[...])
    place = lax.axis_index("red")
    for apart, out_ref in enumerate(out_refs):
        rows = table_ref[pl.ds(pl.multiple_of((place ^ apart) * 16, 16), 16), :]
        for part in range(rows.shape[1] // LANES):
            out_ref[part * wide : (part + 1) * wide, :] = rows[:wide, part * LANES : (part + 1) * LANES]


def right_product(value, matrix_ref):
    high, low = split(value)
    count = value.shape[0]
    both = dot(jnp.concatenate([high, low], axis=0), matrix_ref[0])
    return both[:count] + both[count:] + dot(high, matrix_ref[1])


def conv_kernel(
    scale, in_ref, part_0, part_1, part_2, part_3, first_ref, last_ref, twiddle_ref, forward_ref, backward_ref, out_ref, grads_ref
):
    wide = 3 * OWN
    groups = part_0.shape[0] // wide

    def received(row):
        return in_ref[pl.ds(row, BLOCKS, stride=IN_ROWS), :]

    table = (part_0[...] + part_1[...]) + (part_2[...] + part_3[...])
    ids = received(2 * OWN).astype(jnp.int32)
    lane = ids & (LANES - 1)
    group = ids >> 7

    def looked_up(column):
        value = None
        for g in range(groups):
            row = jnp.broadcast_to(table[g * wide + column : g * wide + column + 1, :], (BLOCKS, LANES))
            found = jnp.take_along_axis(row, lane, axis=1, mode="promise_in_bounds")
            value = found if value is None else jnp.where(group == g, found, value)
        return value

    queries = [looked_up(c) for c in range(OWN)]
    keys = [looked_up(OWN + c) for c in range(OWN)]
    values = [looked_up(2 * OWN + c) for c in range(OWN)]
    cotangent = [received(OWN + c) for c in range(OWN)]
    signals = [received(c) for c in range(OWN)]
    signals += [keys[c] * values[c] for c in range(OWN)]
    signals += [cotangent[c] * queries[c] for c in range(OWN)]
    count = len(signals)

    cosine, sine = twiddle_ref[0], twiddle_ref[1]
    high, low = split(jnp.concatenate(signals, axis=1))
    mixed = dot(first_ref[...], jnp.concatenate([high, low, high], axis=0))
    rows = []
    for n in range(count):
        re = mixed[:BLOCKS, n * LANES : (n + 1) * LANES]
        im = mixed[BLOCKS:, n * LANES : (n + 1) * LANES]
        rows.append(jnp.concatenate([re * cosine + im * sine, im * cosine - re * sine], axis=1))
    spectra = right_product(jnp.concatenate(rows, axis=0), forward_ref)

    def spectrum(n):
        own = spectra[n * BLOCKS : (n + 1) * BLOCKS]
        return own[:, :LANES], own[:, LANES:]

    joined = [None] * count
    for c in range(OWN):
        f_re, f_im = spectrum(c)
        i_re, i_im = spectrum(OWN + c)
        u_re, u_im = spectrum(2 * OWN + c)
        joined[c] = (f_re * i_re - f_im * i_im, f_re * i_im + f_im * i_re)
        joined[OWN + c] = (f_re * u_re + f_im * u_im, f_re * u_im - f_im * u_re)
        joined[2 * OWN + c] = (u_re * i_re + u_im * i_im, u_im * i_re - u_re * i_im)
    back = right_product(
        jnp.concatenate([jnp.concatenate(pair, axis=1) for pair in joined], axis=0), backward_ref
    )
    columns = []
    for n in range(count):
        re = back[n * BLOCKS : (n + 1) * BLOCKS, :LANES]
        im = back[n * BLOCKS : (n + 1) * BLOCKS, LANES:]
        columns.append(jnp.concatenate([re * cosine - im * sine, re * sine + im * cosine], axis=0))
    high, low = split(jnp.concatenate(columns, axis=1))
    result = dot(last_ref[...], jnp.concatenate([high, low, high], axis=0))

    grads_ref[...] = jnp.zeros_like(grads_ref)
    for c in range(OWN):
        conv = result[:, c * LANES : (c + 1) * LANES]
        grad_inner = result[:, (OWN + c) * LANES : (OWN + c + 1) * LANES]
        filter_grad = result[:, (2 * OWN + c) * LANES : (2 * OWN + c + 1) * LANES]
        grads = (cotangent[c] * conv, grad_inner * values[c], grad_inner * keys[c])
        sent = (*grads, queries[c] * conv, filter_grad * scale)
        for number, value in enumerate(sent):
            out_ref[pl.ds(number * OWN + c, BLOCKS, stride=OUT_ROWS), :] = value
        for number, value in enumerate(grads):
            grads_ref[pl.ds(number * OWN + c, BLOCKS, stride=16), :] = value


def sums_kernel(in_ref, grads_ref, out_ref, ids_ref):
    ids_ref[...] = in_ref[pl.ds(2 * OWN, BLOCKS, stride=IN_ROWS), :].astype(jnp.int32)
    groups = out_ref.shape[0] // 16
    total = jnp.zeros(out_ref.shape, F32)
    for pair in range(BLOCKS // 2):
        picked, hot = [], []
        for s in (2 * pair, 2 * pair + 1):
            ids = ids_ref[s : s + 1, :]
            grads = grads_ref[s * 16 : (s + 1) * 16, :]
            group = jnp.broadcast_to(ids >> 7, (16, LANES))
            picked.append(
                jnp.concatenate([jnp.where(group == g, grads, 0.0) for g in range(groups)], axis=0).astype(BF16)
            )
            lane = jnp.broadcast_to(ids & (LANES - 1), (LANES, LANES))
            rows = lax.broadcasted_iota(jnp.int32, (LANES, LANES), 0)
            hot.append(jnp.where(rows == lane, 1.0, 0.0).astype(BF16))
        total = total + dot_last(jnp.concatenate(picked, axis=1), jnp.concatenate(hot, axis=1))
    out_ref[...] = total


def weight_kernel(scale, sums_ref, emb_ref, out_ref):
    branches, reds, piece, _ = out_ref.shape
    groups = sums_ref.shape[1] // 16
    rows = jnp.concatenate(
        [
            jnp.concatenate([sums_ref[q, g * 16 : (g + 1) * 16, :] for g in range(groups)], axis=1)
            for q in range(reds)
        ],
        axis=0,
    )
    high, low = split(rows)
    count = rows.shape[0]
    both = dot(jnp.concatenate([high, low], axis=0), emb_ref[...])
    grad = (both[:count] + both[count:]) * scale
    for q in range(reds):
        for b in range(branches):
            at = q * 16 + b * piece
            out_ref[b, q] = grad[at : at + piece, :]


def unpack_kernel(in_ref, output_ref, filter_ref, branch_ref, turn_ref):
    for number in range(OUT_ROWS // OWN):
        for c in range(OWN):
            turn_ref[number, pl.ds(c, BLOCKS, stride=OWN), :] = in_ref[
                pl.ds(number * OWN + c, BLOCKS, stride=OUT_ROWS), :
            ]
        value = turn_ref[number].T
        if number < 3:
            branch_ref[number] = value.astype(BF16)
        elif number == 3:
            output_ref[...] = value
        else:
            filter_ref[...] = value


def call(body, outs, scratch, *operands, space=pltpu.VMEM, limit=48 * 2**20):
    single = not isinstance(outs, (list, tuple))
    return pl.pallas_call(
        body,
        in_specs=[pl.BlockSpec(memory_space=space)] * len(operands),
        out_shape=outs if single else tuple(outs),
        scratch_shapes=scratch,
        compiler_params=pltpu.CompilerParams(vmem_limit_bytes=limit),
    )(*operands)


def shape(dims, dtype=F32):
    return jax.ShapeDtypeStruct(dims, dtype)


def exchange(value, axis, pieces, rows):
    sent = value.reshape(pieces, 1, rows * LANES)
    got = lax.all_to_all(sent, axis, split_axis=0, concat_axis=0, tiled=True)
    return got.reshape(pieces * rows, LANES)


def shards(token_ids, embedding, proj_weight, filters, cotangent):
    reds = lax.axis_size("red")
    blocks = lax.axis_size("seq")
    width_rows, branches, _, piece = proj_weight.shape
    vocabulary = embedding.shape[0]
    groups = vocabulary // LANES
    positions, channels = filters.shape
    scale = float(positions * blocks) ** (-0.5)

    packed = call(
        pack_kernel,
        shape((BLOCKS * IN_ROWS, LANES)),
        [
            pltpu.VMEM((positions, channels), F32),
            pltpu.VMEM((positions, channels), F32),
            pltpu.VMEM((1, positions), jnp.int32),
            pltpu.VMEM((channels, LANES), F32),
            pltpu.SemaphoreType.DMA((3,)),
        ],
        filters,
        cotangent,
        token_ids.reshape(1, positions),
        space=pl.ANY,
        limit=60 * 2**20,
    )
    arrived = exchange(packed, "seq", BLOCKS, IN_ROWS)
    parts = call(
        table_kernel,
        [shape((groups * branches * piece, LANES))] * reds,
        [pltpu.VMEM((reds * 16, width_rows), F32), pltpu.VMEM((reds * 16, vocabulary), F32)],
        proj_weight.transpose(1, 2, 3, 0),
        embedding,
    )
    parts = [parts[0]] + [
        lax.ppermute(parts[apart], "red", [(q, q ^ apart) for q in range(reds)]) for apart in range(1, reds)
    ]
    constants = [jnp.asarray(c) for c in transform_constants()]
    results, grads = call(
        functools.partial(conv_kernel, scale),
        [shape((BLOCKS * OUT_ROWS, LANES)), shape((BLOCKS * 16, LANES))],
        [],
        arrived,
        *parts,
        *constants,
    )
    returned = exchange(results, "seq", BLOCKS, OUT_ROWS)
    sums = call(
        sums_kernel,
        shape((groups * 16, LANES)),
        [pltpu.VMEM((BLOCKS, LANES), jnp.int32)],
        arrived,
        grads,
    )
    gathered = lax.all_gather(sums, "red", axis=0)
    weight_grad = call(
        functools.partial(weight_kernel, scale),
        shape((branches, reds, piece, width_rows)),
        [],
        gathered,
        embedding,
    )
    output, filter_grad, branch_grads = call(
        unpack_kernel,
        [
            shape((positions, channels)),
            shape((positions, channels)),
            shape((branches, positions, channels), BF16),
        ],
        [pltpu.VMEM((OUT_ROWS // OWN, channels, LANES), F32)],
        returned,
    )
    return output, filter_grad, branch_grads.transpose(1, 0, 2), weight_grad.transpose(3, 0, 1, 2)


def solution(mesh):
    in_specs = (
        P("seq"),
        P(None, "red"),
        P("red", None, None, "seq"),
        P("seq", "red"),
        P("seq", "red"),
    )
    out_specs = (
        P("seq", "red"),
        P("seq", "red"),
        P("seq", None, "red"),
        P("red", None, None, "seq"),
    )
    return jax.shard_map(shards, mesh=mesh, in_specs=in_specs, out_specs=out_specs, check_vma=False)
```

```python
import functools
import math

import jax
import jax.numpy as jnp
import ml_dtypes
import numpy as np
from jax import lax
from jax.experimental import pallas as pl
from jax.experimental.pallas import tpu as pltpu
from jax.sharding import PartitionSpec as P


BLOCKS = 64
LANES = 128
OWN = 4
IN_ROWS = 9
OUT_ROWS = 20
F32 = jnp.float32
BF16 = jnp.bfloat16


def halves(matrix):
    matrix = np.asarray(matrix, np.float32)
    high = matrix.astype(ml_dtypes.bfloat16)
    low = (matrix - high.astype(np.float32)).astype(ml_dtypes.bfloat16)
    return high, low


@functools.cache
def transform_constants():
    odd = np.arange(BLOCKS) + 0.5
    theta = 2.0 * math.pi * np.outer(odd, np.arange(BLOCKS)) / LANES
    rows = np.concatenate([np.cos(theta), -np.sin(theta)], axis=0)
    high, low = halves(rows)
    first = np.concatenate([high, high, low], axis=1)
    high, low = halves(rows.T * (2.0 / (2 * BLOCKS * LANES)))
    last = np.concatenate([high, high, low], axis=1)
    phi = 2.0 * math.pi * np.outer(odd, np.arange(LANES)) / (2 * BLOCKS * LANES)
    twiddle = np.stack([np.cos(phi), np.sin(phi)]).astype(np.float32)
    psi = 2.0 * math.pi * (np.outer(np.arange(LANES), np.arange(LANES)) % LANES) / LANES
    right = np.block([[np.cos(psi), -np.sin(psi)], [np.sin(psi), np.cos(psi)]])
    forward = np.stack(halves(right))
    backward = np.stack(halves(right.T))
    return first, last, twiddle, forward, backward


def split(value):
    high = value.astype(BF16)
    return high, (value - high.astype(F32)).astype(BF16)


def dot(left, right):
    return jnp.dot(left, right, preferred_element_type=F32)


def dot_last(left, right):
    return lax.dot_general(left, right, (((1,), (1,)), ((), ())), preferred_element_type=F32)


def in_blocks_order(in_ref, row):
    halves = [
        in_ref[pl.ds(place * IN_ROWS + row, BLOCKS // 2, stride=IN_ROWS), :] for place in (BLOCKS // 2, 0)
    ]
    return jnp.concatenate(halves, axis=0)


def pack_kernel(filt_hbm, cot_hbm, ids_hbm, out_ref, filt, cot, ids, turn_ref, sems):
    pairs = ((filt_hbm, filt), (cot_hbm, cot), (ids_hbm, ids))
    copies = [pltpu.make_async_copy(source, kept, sems.at[n]) for n, (source, kept) in enumerate(pairs)]
    for copy in copies:
        copy.start()
    for number, ref in enumerate((filt, cot)):
        copies[number].wait()
        turn_ref[...] = ref[...].T
        for c in range(OWN):
            for half in range(2):
                block = half * BLOCKS // 2
                place = (1 - half) * BLOCKS // 2
                out_ref[pl.ds(place * IN_ROWS + number * OWN + c, BLOCKS // 2, stride=IN_ROWS), :] = turn_ref[
                    pl.ds(block * OWN + c, BLOCKS // 2, stride=OWN), :
                ]
    copies[2].wait()
    out_ref[pl.ds(2 * OWN, BLOCKS, stride=IN_ROWS), :] = jnp.broadcast_to(ids[...].astype(F32), (BLOCKS, LANES))


def table_kernel(proj_ref, emb_ref, *refs):
    *out_refs, rows_ref, table_ref = refs
    branches, reds, piece, _ = proj_ref.shape
    wide = branches * piece
    rows_ref[...] = jnp.zeros_like(rows_ref)
    for q in range(reds):
        for b in range(branches):
            at = q * 16 + b * piece
            rows_ref[at : at + piece, :] = proj_ref[b, q].astype(F32)
    table_ref[...] = dot_last(rows_ref[...].astype(BF16), emb_ref[...])
    place = lax.axis_index("red")
    for apart, out_ref in enumerate(out_refs):
        rows = table_ref[pl.ds(pl.multiple_of((place ^ apart) * 16, 16), 16), :]
        for part in range(rows.shape[1] // LANES):
            out_ref[part * wide : (part + 1) * wide, :] = rows[:wide, part * LANES : (part + 1) * LANES]


def right_product(value, matrix_ref):
    high, low = split(value)
    count = value.shape[0]
    both = dot(jnp.concatenate([high, low], axis=0), matrix_ref[0])
    return both[:count] + both[count:] + dot(high, matrix_ref[1])


def conv_kernel(
    scale, in_ref, part_0, part_1, part_2, part_3, first_ref, last_ref, twiddle_ref, forward_ref, backward_ref, out_ref, grads_ref
):
    wide = 3 * OWN
    groups = part_0.shape[0] // wide

    def received(row):
        return in_blocks_order(in_ref, row)

    table = (part_0[...] + part_1[...]) + (part_2[...] + part_3[...])
    ids = received(2 * OWN).astype(jnp.int32)
    lane = ids & (LANES - 1)
    group = ids >> 7

    def looked_up(column):
        value = None
        for g in range(groups):
            row = jnp.broadcast_to(table[g * wide + column : g * wide + column + 1, :], (BLOCKS, LANES))
            found = jnp.take_along_axis(row, lane, axis=1, mode="promise_in_bounds")
            value = found if value is None else jnp.where(group == g, found, value)
        return value

    queries = [looked_up(c) for c in range(OWN)]
    keys = [looked_up(OWN + c) for c in range(OWN)]
    values = [looked_up(2 * OWN + c) for c in range(OWN)]
    cotangent = [received(OWN + c) for c in range(OWN)]
    signals = [received(c) for c in range(OWN)]
    signals += [keys[c] * values[c] for c in range(OWN)]
    signals += [cotangent[c] * queries[c] for c in range(OWN)]
    count = len(signals)

    cosine, sine = twiddle_ref[0], twiddle_ref[1]
    high, low = split(jnp.concatenate(signals, axis=1))
    mixed = dot(first_ref[...], jnp.concatenate([high, low, high], axis=0))
    rows = []
    for n in range(count):
        re = mixed[:BLOCKS, n * LANES : (n + 1) * LANES]
        im = mixed[BLOCKS:, n * LANES : (n + 1) * LANES]
        rows.append(jnp.concatenate([re * cosine + im * sine, im * cosine - re * sine], axis=1))
    spectra = right_product(jnp.concatenate(rows, axis=0), forward_ref)

    def spectrum(n):
        own = spectra[n * BLOCKS : (n + 1) * BLOCKS]
        return own[:, :LANES], own[:, LANES:]

    joined = [None] * count
    for c in range(OWN):
        f_re, f_im = spectrum(c)
        i_re, i_im = spectrum(OWN + c)
        u_re, u_im = spectrum(2 * OWN + c)
        joined[c] = (f_re * i_re - f_im * i_im, f_re * i_im + f_im * i_re)
        joined[OWN + c] = (f_re * u_re + f_im * u_im, f_re * u_im - f_im * u_re)
        joined[2 * OWN + c] = (u_re * i_re + u_im * i_im, u_im * i_re - u_re * i_im)
    back = right_product(
        jnp.concatenate([jnp.concatenate(pair, axis=1) for pair in joined], axis=0), backward_ref
    )
    columns = []
    for n in range(count):
        re = back[n * BLOCKS : (n + 1) * BLOCKS, :LANES]
        im = back[n * BLOCKS : (n + 1) * BLOCKS, LANES:]
        columns.append(jnp.concatenate([re * cosine - im * sine, re * sine + im * cosine], axis=0))
    high, low = split(jnp.concatenate(columns, axis=1))
    result = dot(last_ref[...], jnp.concatenate([high, low, high], axis=0))

    grads_ref[...] = jnp.zeros_like(grads_ref)
    for c in range(OWN):
        conv = result[:, c * LANES : (c + 1) * LANES]
        grad_inner = result[:, (OWN + c) * LANES : (OWN + c + 1) * LANES]
        filter_grad = result[:, (2 * OWN + c) * LANES : (2 * OWN + c + 1) * LANES]
        grads = (cotangent[c] * conv, grad_inner * values[c], grad_inner * keys[c])
        sent = (*grads, queries[c] * conv, filter_grad * scale)
        for number, value in enumerate(sent):
            out_ref[pl.ds(number * OWN + c, BLOCKS, stride=OUT_ROWS), :] = value
        for number, value in enumerate(grads):
            grads_ref[pl.ds(number * OWN + c, BLOCKS, stride=16), :] = value


def sums_kernel(in_ref, grads_ref, out_ref, ids_ref):
    ids_ref[...] = in_blocks_order(in_ref, 2 * OWN).astype(jnp.int32)
    groups = out_ref.shape[0] // 16
    total = jnp.zeros(out_ref.shape, F32)
    for pair in range(BLOCKS // 2):
        picked, hot = [], []
        for s in (2 * pair, 2 * pair + 1):
            ids = ids_ref[s : s + 1, :]
            grads = grads_ref[s * 16 : (s + 1) * 16, :]
            group = jnp.broadcast_to(ids >> 7, (16, LANES))
            picked.append(
                jnp.concatenate([jnp.where(group == g, grads, 0.0) for g in range(groups)], axis=0).astype(BF16)
            )
            lane = jnp.broadcast_to(ids & (LANES - 1), (LANES, LANES))
            rows = lax.broadcasted_iota(jnp.int32, (LANES, LANES), 0)
            hot.append(jnp.where(rows == lane, 1.0, 0.0).astype(BF16))
        total = total + dot_last(jnp.concatenate(picked, axis=1), jnp.concatenate(hot, axis=1))
    out_ref[...] = total


def weight_kernel(scale, sums_ref, emb_ref, out_ref):
    branches, reds, piece, _ = out_ref.shape
    groups = sums_ref.shape[1] // 16
    rows = jnp.concatenate(
        [
            jnp.concatenate([sums_ref[q, g * 16 : (g + 1) * 16, :] for g in range(groups)], axis=1)
            for q in range(reds)
        ],
        axis=0,
    )
    high, low = split(rows)
    count = rows.shape[0]
    both = dot(jnp.concatenate([high, low], axis=0), emb_ref[...])
    grad = (both[:count] + both[count:]) * scale
    for q in range(reds):
        for b in range(branches):
            at = q * 16 + b * piece
            out_ref[b, q] = grad[at : at + piece, :]


def unpack_kernel(in_ref, output_ref, filter_ref, branch_ref, turn_ref):
    for number in range(OUT_ROWS // OWN):
        for c in range(OWN):
            turn_ref[number, pl.ds(c, BLOCKS, stride=OWN), :] = in_ref[
                pl.ds(number * OWN + c, BLOCKS, stride=OUT_ROWS), :
            ]
        value = turn_ref[number].T
        if number < 3:
            branch_ref[number] = value.astype(BF16)
        elif number == 3:
            output_ref[...] = value
        else:
            filter_ref[...] = value


def call(body, outs, scratch, *operands, space=pltpu.VMEM, limit=48 * 2**20):
    single = not isinstance(outs, (list, tuple))
    return pl.pallas_call(
        body,
        in_specs=[pl.BlockSpec(memory_space=space)] * len(operands),
        out_shape=outs if single else tuple(outs),
        scratch_shapes=scratch,
        compiler_params=pltpu.CompilerParams(vmem_limit_bytes=limit),
    )(*operands)


def shape(dims, dtype=F32):
    return jax.ShapeDtypeStruct(dims, dtype)


def exchange(value, axis, pieces, rows, first=0):
    order = [(first + place) % pieces for place in range(pieces)]
    sent = value.reshape(pieces, 1, rows * LANES)
    got = lax.all_to_all(sent, axis, split_axis=0, concat_axis=0, tiled=True, axis_index_groups=[order])
    return got.reshape(pieces * rows, LANES)


def shards(token_ids, embedding, proj_weight, filters, cotangent):
    reds = lax.axis_size("red")
    blocks = lax.axis_size("seq")
    width_rows, branches, _, piece = proj_weight.shape
    vocabulary = embedding.shape[0]
    groups = vocabulary // LANES
    positions, channels = filters.shape
    scale = float(positions * blocks) ** (-0.5)

    packed = call(
        pack_kernel,
        shape((BLOCKS * IN_ROWS, LANES)),
        [
            pltpu.VMEM((positions, channels), F32),
            pltpu.VMEM((positions, channels), F32),
            pltpu.VMEM((1, positions), jnp.int32),
            pltpu.VMEM((channels, LANES), F32),
            pltpu.SemaphoreType.DMA((3,)),
        ],
        filters,
        cotangent,
        token_ids.reshape(1, positions),
        space=pl.ANY,
        limit=60 * 2**20,
    )
    arrived = exchange(packed, "seq", BLOCKS, IN_ROWS, first=BLOCKS // 2)
    parts = call(
        table_kernel,
        [shape((groups * branches * piece, LANES))] * reds,
        [pltpu.VMEM((reds * 16, width_rows), F32), pltpu.VMEM((reds * 16, vocabulary), F32)],
        proj_weight.transpose(1, 2, 3, 0),
        embedding,
    )
    parts = [parts[0]] + [
        lax.ppermute(parts[apart], "red", [(q, q ^ apart) for q in range(reds)]) for apart in range(1, reds)
    ]
    constants = [jnp.asarray(c) for c in transform_constants()]
    results, grads = call(
        functools.partial(conv_kernel, scale),
        [shape((BLOCKS * OUT_ROWS, LANES)), shape((BLOCKS * 16, LANES))],
        [],
        arrived,
        *parts,
        *constants,
    )
    returned = exchange(results, "seq", BLOCKS, OUT_ROWS)
    sums = call(
        sums_kernel,
        shape((groups * 16, LANES)),
        [pltpu.VMEM((BLOCKS, LANES), jnp.int32)],
        arrived,
        grads,
    )
    gathered = lax.all_gather(sums, "red", axis=0)
    weight_grad = call(
        functools.partial(weight_kernel, scale),
        shape((branches, reds, piece, width_rows)),
        [],
        gathered,
        embedding,
    )
    output, filter_grad, branch_grads = call(
        unpack_kernel,
        [
            shape((positions, channels)),
            shape((positions, channels)),
            shape((branches, positions, channels), BF16),
        ],
        [pltpu.VMEM((OUT_ROWS // OWN, channels, LANES), F32)],
        returned,
    )
    return output, filter_grad, branch_grads.transpose(1, 0, 2), weight_grad.transpose(3, 0, 1, 2)


def solution(mesh):
    in_specs = (
        P("seq"),
        P(None, "red"),
        P("red", None, None, "seq"),
        P("seq", "red"),
        P("seq", "red"),
    )
    out_specs = (
        P("seq", "red"),
        P("seq", "red"),
        P("seq", None, "red"),
        P("red", None, None, "seq"),
    )
    return jax.shard_map(shards, mesh=mesh, in_specs=in_specs, out_specs=out_specs, check_vma=False)
```

```python
import functools
import math

import jax
import jax.numpy as jnp
import ml_dtypes
import numpy as np
from jax import lax
from jax.experimental import pallas as pl
from jax.experimental.pallas import tpu as pltpu
from jax.sharding import PartitionSpec as P


BLOCKS = 64
PLANE = 16
LANES = 128
OWN = 4
IN_ROWS = 9
OUT_ROWS = 20
F32 = jnp.float32
BF16 = jnp.bfloat16


def halves(matrix):
    matrix = np.asarray(matrix, np.float32)
    high = matrix.astype(ml_dtypes.bfloat16)
    low = (matrix - high.astype(np.float32)).astype(ml_dtypes.bfloat16)
    return high, low


@functools.cache
def transform_constants():
    odd = np.arange(BLOCKS) + 0.5
    theta = 2.0 * math.pi * np.outer(odd, np.arange(BLOCKS)) / LANES
    rows = np.concatenate([np.cos(theta), -np.sin(theta)], axis=0)
    high, low = halves(rows)
    first = np.concatenate([high, high, low], axis=1)
    high, low = halves(rows.T * (2.0 / (2 * BLOCKS * LANES)))
    last = np.concatenate([high, high, low], axis=1)
    phi = 2.0 * math.pi * np.outer(odd, np.arange(LANES)) / (2 * BLOCKS * LANES)
    twiddle = np.stack([np.cos(phi), np.sin(phi)]).astype(np.float32)
    psi = 2.0 * math.pi * (np.outer(np.arange(LANES), np.arange(LANES)) % LANES) / LANES
    right = np.block([[np.cos(psi), -np.sin(psi)], [np.sin(psi), np.cos(psi)]])
    forward = np.stack(halves(right))
    backward = np.stack(halves(right.T))
    return first, last, twiddle, forward, backward


def split(value):
    high = value.astype(BF16)
    return high, (value - high.astype(F32)).astype(BF16)


def dot(left, right):
    return jnp.dot(left, right, preferred_element_type=F32)


def dot_last(left, right):
    return lax.dot_general(left, right, (((1,), (1,)), ((), ())), preferred_element_type=F32)


def in_blocks_order(in_ref, row):
    halves = [
        in_ref[pl.ds(place * IN_ROWS + row, BLOCKS // 2, stride=IN_ROWS), :] for place in (BLOCKS // 2, 0)
    ]
    return jnp.concatenate(halves, axis=0)


def planes_reversed(value):
    return jnp.concatenate([value[at : at + PLANE] for at in range(BLOCKS - PLANE, -1, -PLANE)], axis=0)


def pack_kernel(filt_hbm, cot_hbm, ids_hbm, out_ref, filt, cot, ids, turn_ref, sems):
    pairs = ((filt_hbm, filt), (cot_hbm, cot), (ids_hbm, ids))
    copies = [pltpu.make_async_copy(source, kept, sems.at[n]) for n, (source, kept) in enumerate(pairs)]
    for copy in copies:
        copy.start()
    for number, ref in enumerate((filt, cot)):
        copies[number].wait()
        turn_ref[...] = ref[...].T
        for c in range(OWN):
            for half in range(2):
                block = half * BLOCKS // 2
                place = (1 - half) * BLOCKS // 2
                out_ref[pl.ds(place * IN_ROWS + number * OWN + c, BLOCKS // 2, stride=IN_ROWS), :] = turn_ref[
                    pl.ds(block * OWN + c, BLOCKS // 2, stride=OWN), :
                ]
    copies[2].wait()
    out_ref[pl.ds(2 * OWN, BLOCKS, stride=IN_ROWS), :] = jnp.broadcast_to(ids[...].astype(F32), (BLOCKS, LANES))


def table_kernel(proj_ref, emb_ref, *refs):
    *out_refs, rows_ref, table_ref = refs
    branches, reds, piece, _ = proj_ref.shape
    wide = branches * piece
    rows_ref[...] = jnp.zeros_like(rows_ref)
    for q in range(reds):
        for b in range(branches):
            at = q * 16 + b * piece
            rows_ref[at : at + piece, :] = proj_ref[b, q].astype(F32)
    table_ref[...] = dot_last(rows_ref[...].astype(BF16), emb_ref[...])
    place = lax.axis_index("red")
    for apart, out_ref in enumerate(out_refs):
        rows = table_ref[pl.ds(pl.multiple_of((place ^ apart) * 16, 16), 16), :]
        for part in range(rows.shape[1] // LANES):
            out_ref[part * wide : (part + 1) * wide, :] = rows[:wide, part * LANES : (part + 1) * LANES]


def right_product(value, matrix_ref):
    high, low = split(value)
    count = value.shape[0]
    both = dot(jnp.concatenate([high, low], axis=0), matrix_ref[0])
    return both[:count] + both[count:] + dot(high, matrix_ref[1])


def conv_kernel(
    scale, in_ref, part_0, part_1, part_2, part_3, first_ref, last_ref, twiddle_ref, forward_ref, backward_ref, out_ref, grads_ref
):
    wide = 3 * OWN
    groups = part_0.shape[0] // wide

    def received(row):
        return in_blocks_order(in_ref, row)

    table = (part_0[...] + part_1[...]) + (part_2[...] + part_3[...])
    ids = received(2 * OWN).astype(jnp.int32)
    lane = ids & (LANES - 1)
    group = ids >> 7

    def looked_up(column):
        value = None
        for g in range(groups):
            row = jnp.broadcast_to(table[g * wide + column : g * wide + column + 1, :], (BLOCKS, LANES))
            found = jnp.take_along_axis(row, lane, axis=1, mode="promise_in_bounds")
            value = found if value is None else jnp.where(group == g, found, value)
        return value

    queries = [looked_up(c) for c in range(OWN)]
    keys = [looked_up(OWN + c) for c in range(OWN)]
    values = [looked_up(2 * OWN + c) for c in range(OWN)]
    cotangent = [received(OWN + c) for c in range(OWN)]
    signals = [received(c) for c in range(OWN)]
    signals += [keys[c] * values[c] for c in range(OWN)]
    signals += [cotangent[c] * queries[c] for c in range(OWN)]
    count = len(signals)

    cosine, sine = twiddle_ref[0], twiddle_ref[1]
    high, low = split(jnp.concatenate(signals, axis=1))
    mixed = dot(first_ref[...], jnp.concatenate([high, low, high], axis=0))
    rows = []
    for n in range(count):
        re = mixed[:BLOCKS, n * LANES : (n + 1) * LANES]
        im = mixed[BLOCKS:, n * LANES : (n + 1) * LANES]
        rows.append(jnp.concatenate([re * cosine + im * sine, im * cosine - re * sine], axis=1))
    spectra = right_product(jnp.concatenate(rows, axis=0), forward_ref)

    def spectrum(n):
        own = spectra[n * BLOCKS : (n + 1) * BLOCKS]
        return own[:, :LANES], own[:, LANES:]

    joined = [None] * count
    for c in range(OWN):
        f_re, f_im = spectrum(c)
        i_re, i_im = spectrum(OWN + c)
        u_re, u_im = spectrum(2 * OWN + c)
        joined[c] = (f_re * i_re - f_im * i_im, f_re * i_im + f_im * i_re)
        joined[OWN + c] = (f_re * u_re + f_im * u_im, f_re * u_im - f_im * u_re)
        joined[2 * OWN + c] = (u_re * i_re + u_im * i_im, u_im * i_re - u_re * i_im)
    back = right_product(
        jnp.concatenate([jnp.concatenate(pair, axis=1) for pair in joined], axis=0), backward_ref
    )
    columns = []
    for n in range(count):
        re = back[n * BLOCKS : (n + 1) * BLOCKS, :LANES]
        im = back[n * BLOCKS : (n + 1) * BLOCKS, LANES:]
        columns.append(jnp.concatenate([re * cosine - im * sine, re * sine + im * cosine], axis=0))
    high, low = split(jnp.concatenate(columns, axis=1))
    result = dot(last_ref[...], jnp.concatenate([high, low, high], axis=0))

    grads_ref[...] = jnp.zeros_like(grads_ref)
    for c in range(OWN):
        conv = result[:, c * LANES : (c + 1) * LANES]
        grad_inner = result[:, (OWN + c) * LANES : (OWN + c + 1) * LANES]
        filter_grad = result[:, (2 * OWN + c) * LANES : (2 * OWN + c + 1) * LANES]
        grads = (cotangent[c] * conv, grad_inner * values[c], grad_inner * keys[c])
        sent = (*grads, queries[c] * conv, filter_grad * scale)
        for number, value in enumerate(sent):
            out_ref[pl.ds(number * OWN + c, BLOCKS, stride=OUT_ROWS), :] = planes_reversed(value)
        for number, value in enumerate(grads):
            grads_ref[pl.ds(number * OWN + c, BLOCKS, stride=16), :] = value


def sums_kernel(in_ref, grads_ref, out_ref, ids_ref):
    ids_ref[...] = in_blocks_order(in_ref, 2 * OWN).astype(jnp.int32)
    groups = out_ref.shape[0] // 16
    total = jnp.zeros(out_ref.shape, F32)
    for pair in range(BLOCKS // 2):
        picked, hot = [], []
        for s in (2 * pair, 2 * pair + 1):
            ids = ids_ref[s : s + 1, :]
            grads = grads_ref[s * 16 : (s + 1) * 16, :]
            group = jnp.broadcast_to(ids >> 7, (16, LANES))
            picked.append(
                jnp.concatenate([jnp.where(group == g, grads, 0.0) for g in range(groups)], axis=0).astype(BF16)
            )
            lane = jnp.broadcast_to(ids & (LANES - 1), (LANES, LANES))
            rows = lax.broadcasted_iota(jnp.int32, (LANES, LANES), 0)
            hot.append(jnp.where(rows == lane, 1.0, 0.0).astype(BF16))
        total = total + dot_last(jnp.concatenate(picked, axis=1), jnp.concatenate(hot, axis=1))
    out_ref[...] = total


def weight_kernel(scale, sums_ref, emb_ref, out_ref):
    branches, reds, piece, _ = out_ref.shape
    groups = sums_ref.shape[1] // 16
    rows = jnp.concatenate(
        [
            jnp.concatenate([sums_ref[q, g * 16 : (g + 1) * 16, :] for g in range(groups)], axis=1)
            for q in range(reds)
        ],
        axis=0,
    )
    high, low = split(rows)
    count = rows.shape[0]
    both = dot(jnp.concatenate([high, low], axis=0), emb_ref[...])
    grad = (both[:count] + both[count:]) * scale
    for q in range(reds):
        for b in range(branches):
            at = q * 16 + b * piece
            out_ref[b, q] = grad[at : at + piece, :]


def unpack_kernel(in_ref, output_ref, filter_ref, branch_ref, turn_ref):
    for number in range(OUT_ROWS // OWN):
        for c in range(OWN):
            turn_ref[number, pl.ds(c, BLOCKS, stride=OWN), :] = planes_reversed(
                in_ref[pl.ds(number * OWN + c, BLOCKS, stride=OUT_ROWS), :]
            )
        value = turn_ref[number].T
        if number < 3:
            branch_ref[number] = value.astype(BF16)
        elif number == 3:
            output_ref[...] = value
        else:
            filter_ref[...] = value


def call(body, outs, scratch, *operands, space=pltpu.VMEM, limit=48 * 2**20):
    single = not isinstance(outs, (list, tuple))
    return pl.pallas_call(
        body,
        in_specs=[pl.BlockSpec(memory_space=space)] * len(operands),
        out_shape=outs if single else tuple(outs),
        scratch_shapes=scratch,
        compiler_params=pltpu.CompilerParams(vmem_limit_bytes=limit),
    )(*operands)


def shape(dims, dtype=F32):
    return jax.ShapeDtypeStruct(dims, dtype)


def exchange(value, axis, pieces, rows, order):
    sent = value.reshape(pieces, 1, rows * LANES)
    got = lax.all_to_all(sent, axis, split_axis=0, concat_axis=0, tiled=True, axis_index_groups=[list(order)])
    return got.reshape(pieces * rows, LANES)


def shards(token_ids, embedding, proj_weight, filters, cotangent):
    reds = lax.axis_size("red")
    blocks = lax.axis_size("seq")
    width_rows, branches, _, piece = proj_weight.shape
    vocabulary = embedding.shape[0]
    groups = vocabulary // LANES
    positions, channels = filters.shape
    scale = float(positions * blocks) ** (-0.5)
    numbers = np.arange(BLOCKS)

    packed = call(
        pack_kernel,
        shape((BLOCKS * IN_ROWS, LANES)),
        [
            pltpu.VMEM((positions, channels), F32),
            pltpu.VMEM((positions, channels), F32),
            pltpu.VMEM((1, positions), jnp.int32),
            pltpu.VMEM((channels, LANES), F32),
            pltpu.SemaphoreType.DMA((3,)),
        ],
        filters,
        cotangent,
        token_ids.reshape(1, positions),
        space=pl.ANY,
        limit=60 * 2**20,
    )
    arrived = exchange(packed, "seq", BLOCKS, IN_ROWS, np.roll(numbers, BLOCKS // 2).tolist())
    parts = call(
        table_kernel,
        [shape((groups * branches * piece, LANES))] * reds,
        [pltpu.VMEM((reds * 16, width_rows), F32), pltpu.VMEM((reds * 16, vocabulary), F32)],
        proj_weight.transpose(1, 2, 3, 0),
        embedding,
    )
    parts = [parts[0]] + [
        lax.ppermute(parts[apart], "red", [(q, q ^ apart) for q in range(reds)]) for apart in range(1, reds)
    ]
    constants = [jnp.asarray(c) for c in transform_constants()]
    results, grads = call(
        functools.partial(conv_kernel, scale),
        [shape((BLOCKS * OUT_ROWS, LANES)), shape((BLOCKS * 16, LANES))],
        [],
        arrived,
        *parts,
        *constants,
    )
    returned = exchange(results, "seq", BLOCKS, OUT_ROWS, numbers.reshape(-1, PLANE)[::-1].ravel().tolist())
    sums = call(
        sums_kernel,
        shape((groups * 16, LANES)),
        [pltpu.VMEM((BLOCKS, LANES), jnp.int32)],
        arrived,
        grads,
    )
    gathered = lax.all_gather(sums, "red", axis=0)
    weight_grad = call(
        functools.partial(weight_kernel, scale),
        shape((branches, reds, piece, width_rows)),
        [],
        gathered,
        embedding,
    )
    output, filter_grad, branch_grads = call(
        unpack_kernel,
        [
            shape((positions, channels)),
            shape((positions, channels)),
            shape((branches, positions, channels), BF16),
        ],
        [pltpu.VMEM((OUT_ROWS // OWN, channels, LANES), F32)],
        returned,
    )
    return output, filter_grad, branch_grads.transpose(1, 0, 2), weight_grad.transpose(3, 0, 1, 2)


def solution(mesh):
    in_specs = (
        P("seq"),
        P(None, "red"),
        P("red", None, None, "seq"),
        P("seq", "red"),
        P("seq", "red"),
    )
    out_specs = (
        P("seq", "red"),
        P("seq", "red"),
        P("seq", None, "red"),
        P("red", None, None, "seq"),
    )
    return jax.shard_map(shards, mesh=mesh, in_specs=in_specs, out_specs=out_specs, check_vma=False)
```

```python
import functools
import math

import jax
import jax.numpy as jnp
import ml_dtypes
import numpy as np
from jax import lax
from jax.experimental import pallas as pl
from jax.experimental.pallas import tpu as pltpu
from jax.sharding import PartitionSpec as P


BLOCKS = 64
PLANE = 16
LANES = 128
OWN = 4
IN_ROWS = 9
OUT_ROWS = 20
F32 = jnp.float32
BF16 = jnp.bfloat16


def halves(matrix):
    matrix = np.asarray(matrix, np.float32)
    high = matrix.astype(ml_dtypes.bfloat16)
    low = (matrix - high.astype(np.float32)).astype(ml_dtypes.bfloat16)
    return high, low


@functools.cache
def transform_constants():
    odd = np.arange(BLOCKS) + 0.5
    theta = 2.0 * math.pi * np.outer(odd, np.arange(BLOCKS)) / LANES
    rows = np.concatenate([np.cos(theta), -np.sin(theta)], axis=0)
    high, low = halves(rows)
    first = np.concatenate([high, high, low], axis=1)
    high, low = halves(rows.T * (2.0 / (2 * BLOCKS * LANES)))
    last = np.concatenate([high, high, low], axis=1)
    phi = 2.0 * math.pi * np.outer(odd, np.arange(LANES)) / (2 * BLOCKS * LANES)
    twiddle = np.stack([np.cos(phi), np.sin(phi)]).astype(np.float32)
    psi = 2.0 * math.pi * (np.outer(np.arange(LANES), np.arange(LANES)) % LANES) / LANES
    right = np.block([[np.cos(psi), -np.sin(psi)], [np.sin(psi), np.cos(psi)]])
    forward = np.stack(halves(right))
    backward = np.stack(halves(right.T))
    return first, last, twiddle, forward, backward


def split(value):
    high = value.astype(BF16)
    return high, (value - high.astype(F32)).astype(BF16)


def dot(left, right):
    return jnp.dot(left, right, preferred_element_type=F32)


def dot_last(left, right):
    return lax.dot_general(left, right, (((1,), (1,)), ((), ())), preferred_element_type=F32)


def in_blocks_order(in_ref, row):
    halves = [
        in_ref[pl.ds(place * IN_ROWS + row, BLOCKS // 2, stride=IN_ROWS), :] for place in (BLOCKS // 2, 0)
    ]
    return jnp.concatenate(halves, axis=0)


def planes_reversed(value):
    return jnp.concatenate([value[at : at + PLANE] for at in range(BLOCKS - PLANE, -1, -PLANE)], axis=0)


def pack_kernel(filt_hbm, cot_hbm, ids_hbm, out_ref, filt, cot, ids, turn_ref, sems):
    pairs = ((filt_hbm, filt), (cot_hbm, cot), (ids_hbm, ids))
    copies = [pltpu.make_async_copy(source, kept, sems.at[n]) for n, (source, kept) in enumerate(pairs)]
    for copy in copies:
        copy.start()
    for number, ref in enumerate((filt, cot)):
        copies[number].wait()
        turn_ref[...] = ref[...].T
        for c in range(OWN):
            for half in range(2):
                block = half * BLOCKS // 2
                place = (1 - half) * BLOCKS // 2
                out_ref[pl.ds(place * IN_ROWS + number * OWN + c, BLOCKS // 2, stride=IN_ROWS), :] = turn_ref[
                    pl.ds(block * OWN + c, BLOCKS // 2, stride=OWN), :
                ]
    copies[2].wait()
    out_ref[pl.ds(2 * OWN, BLOCKS, stride=IN_ROWS), :] = jnp.broadcast_to(ids[...].astype(F32), (BLOCKS, LANES))


def table_kernel(proj_ref, emb_ref, *refs):
    *out_refs, rows_ref, table_ref = refs
    branches, reds, piece, _ = proj_ref.shape
    wide = branches * piece
    rows_ref[...] = jnp.zeros_like(rows_ref)
    for q in range(reds):
        for b in range(branches):
            at = q * 16 + b * piece
            rows_ref[at : at + piece, :] = proj_ref[b, q].astype(F32)
    table_ref[...] = dot_last(rows_ref[...].astype(BF16), emb_ref[...])
    place = lax.axis_index("red")
    own_ref, pair_ref, across_ref = out_refs
    held = across_ref.shape[0]
    for apart, out_ref, base in ((0, own_ref, 0), (1, pair_ref, 0), (3, pair_ref, held), (2, across_ref, 0)):
        rows = table_ref[pl.ds(pl.multiple_of((place ^ apart) * 16, 16), 16), :]
        for part in range(rows.shape[1] // LANES):
            at = base + part * wide
            out_ref[at : at + wide, :] = rows[:wide, part * LANES : (part + 1) * LANES]


def right_product(value, matrix_ref):
    high, low = split(value)
    count = value.shape[0]
    both = dot(jnp.concatenate([high, low], axis=0), matrix_ref[0])
    return both[:count] + both[count:] + dot(high, matrix_ref[1])


def conv_kernel(
    scale, in_ref, part_0, part_1, part_2, first_ref, last_ref, twiddle_ref, forward_ref, backward_ref, out_ref, grads_ref
):
    wide = 3 * OWN
    groups = part_0.shape[0] // wide

    def received(row):
        return in_blocks_order(in_ref, row)

    table = (part_0[...] + part_1[: part_0.shape[0]]) + part_2[...]
    ids = received(2 * OWN).astype(jnp.int32)
    lane = ids & (LANES - 1)
    group = ids >> 7

    def looked_up(column):
        value = None
        for g in range(groups):
            row = jnp.broadcast_to(table[g * wide + column : g * wide + column + 1, :], (BLOCKS, LANES))
            found = jnp.take_along_axis(row, lane, axis=1, mode="promise_in_bounds")
            value = found if value is None else jnp.where(group == g, found, value)
        return value

    queries = [looked_up(c) for c in range(OWN)]
    keys = [looked_up(OWN + c) for c in range(OWN)]
    values = [looked_up(2 * OWN + c) for c in range(OWN)]
    cotangent = [received(OWN + c) for c in range(OWN)]
    signals = [received(c) for c in range(OWN)]
    signals += [keys[c] * values[c] for c in range(OWN)]
    signals += [cotangent[c] * queries[c] for c in range(OWN)]
    count = len(signals)

    cosine, sine = twiddle_ref[0], twiddle_ref[1]
    high, low = split(jnp.concatenate(signals, axis=1))
    mixed = dot(first_ref[...], jnp.concatenate([high, low, high], axis=0))
    rows = []
    for n in range(count):
        re = mixed[:BLOCKS, n * LANES : (n + 1) * LANES]
        im = mixed[BLOCKS:, n * LANES : (n + 1) * LANES]
        rows.append(jnp.concatenate([re * cosine + im * sine, im * cosine - re * sine], axis=1))
    spectra = right_product(jnp.concatenate(rows, axis=0), forward_ref)

    def spectrum(n):
        own = spectra[n * BLOCKS : (n + 1) * BLOCKS]
        return own[:, :LANES], own[:, LANES:]

    joined = [None] * count
    for c in range(OWN):
        f_re, f_im = spectrum(c)
        i_re, i_im = spectrum(OWN + c)
        u_re, u_im = spectrum(2 * OWN + c)
        joined[c] = (f_re * i_re - f_im * i_im, f_re * i_im + f_im * i_re)
        joined[OWN + c] = (f_re * u_re + f_im * u_im, f_re * u_im - f_im * u_re)
        joined[2 * OWN + c] = (u_re * i_re + u_im * i_im, u_im * i_re - u_re * i_im)
    back = right_product(
        jnp.concatenate([jnp.concatenate(pair, axis=1) for pair in joined], axis=0), backward_ref
    )
    columns = []
    for n in range(count):
        re = back[n * BLOCKS : (n + 1) * BLOCKS, :LANES]
        im = back[n * BLOCKS : (n + 1) * BLOCKS, LANES:]
        columns.append(jnp.concatenate([re * cosine - im * sine, re * sine + im * cosine], axis=0))
    high, low = split(jnp.concatenate(columns, axis=1))
    result = dot(last_ref[...], jnp.concatenate([high, low, high], axis=0))

    grads_ref[...] = jnp.zeros_like(grads_ref)
    for c in range(OWN):
        conv = result[:, c * LANES : (c + 1) * LANES]
        grad_inner = result[:, (OWN + c) * LANES : (OWN + c + 1) * LANES]
        filter_grad = result[:, (2 * OWN + c) * LANES : (2 * OWN + c + 1) * LANES]
        grads = (cotangent[c] * conv, grad_inner * values[c], grad_inner * keys[c])
        sent = (*grads, queries[c] * conv, filter_grad * scale)
        for number, value in enumerate(sent):
            out_ref[pl.ds(number * OWN + c, BLOCKS, stride=OUT_ROWS), :] = planes_reversed(value)
        for number, value in enumerate(grads):
            grads_ref[pl.ds(number * OWN + c, BLOCKS, stride=16), :] = value


def sums_kernel(in_ref, grads_ref, out_ref, ids_ref):
    ids_ref[...] = in_blocks_order(in_ref, 2 * OWN).astype(jnp.int32)
    groups = out_ref.shape[0] // 16
    total = jnp.zeros(out_ref.shape, F32)
    for pair in range(BLOCKS // 2):
        picked, hot = [], []
        for s in (2 * pair, 2 * pair + 1):
            ids = ids_ref[s : s + 1, :]
            grads = grads_ref[s * 16 : (s + 1) * 16, :]
            group = jnp.broadcast_to(ids >> 7, (16, LANES))
            picked.append(
                jnp.concatenate([jnp.where(group == g, grads, 0.0) for g in range(groups)], axis=0).astype(BF16)
            )
            lane = jnp.broadcast_to(ids & (LANES - 1), (LANES, LANES))
            rows = lax.broadcasted_iota(jnp.int32, (LANES, LANES), 0)
            hot.append(jnp.where(rows == lane, 1.0, 0.0).astype(BF16))
        total = total + dot_last(jnp.concatenate(picked, axis=1), jnp.concatenate(hot, axis=1))
    out_ref[...] = total


def weight_kernel(scale, sums_ref, emb_ref, out_ref):
    branches, reds, piece, _ = out_ref.shape
    groups = sums_ref.shape[1] // 16
    rows = jnp.concatenate(
        [
            jnp.concatenate([sums_ref[q, g * 16 : (g + 1) * 16, :] for g in range(groups)], axis=1)
            for q in range(reds)
        ],
        axis=0,
    )
    high, low = split(rows)
    count = rows.shape[0]
    both = dot(jnp.concatenate([high, low], axis=0), emb_ref[...])
    grad = (both[:count] + both[count:]) * scale
    for q in range(reds):
        for b in range(branches):
            at = q * 16 + b * piece
            out_ref[b, q] = grad[at : at + piece, :]


def unpack_kernel(in_ref, output_ref, filter_ref, branch_ref, turn_ref):
    for number in range(OUT_ROWS // OWN):
        for c in range(OWN):
            turn_ref[number, pl.ds(c, BLOCKS, stride=OWN), :] = planes_reversed(
                in_ref[pl.ds(number * OWN + c, BLOCKS, stride=OUT_ROWS), :]
            )
        value = turn_ref[number].T
        if number < 3:
            branch_ref[number] = value.astype(BF16)
        elif number == 3:
            output_ref[...] = value
        else:
            filter_ref[...] = value


def call(body, outs, scratch, *operands, space=pltpu.VMEM, limit=48 * 2**20):
    single = not isinstance(outs, (list, tuple))
    return pl.pallas_call(
        body,
        in_specs=[pl.BlockSpec(memory_space=space)] * len(operands),
        out_shape=outs if single else tuple(outs),
        scratch_shapes=scratch,
        compiler_params=pltpu.CompilerParams(vmem_limit_bytes=limit),
    )(*operands)


def shape(dims, dtype=F32):
    return jax.ShapeDtypeStruct(dims, dtype)


def exchange(value, axis, pieces, rows, order):
    sent = value.reshape(pieces, 1, rows * LANES)
    got = lax.all_to_all(sent, axis, split_axis=0, concat_axis=0, tiled=True, axis_index_groups=[list(order)])
    return got.reshape(pieces * rows, LANES)


def shards(token_ids, embedding, proj_weight, filters, cotangent):
    reds = lax.axis_size("red")
    blocks = lax.axis_size("seq")
    width_rows, branches, _, piece = proj_weight.shape
    vocabulary = embedding.shape[0]
    groups = vocabulary // LANES
    positions, channels = filters.shape
    scale = float(positions * blocks) ** (-0.5)
    numbers = np.arange(BLOCKS)

    packed = call(
        pack_kernel,
        shape((BLOCKS * IN_ROWS, LANES)),
        [
            pltpu.VMEM((positions, channels), F32),
            pltpu.VMEM((positions, channels), F32),
            pltpu.VMEM((1, positions), jnp.int32),
            pltpu.VMEM((channels, LANES), F32),
            pltpu.SemaphoreType.DMA((3,)),
        ],
        filters,
        cotangent,
        token_ids.reshape(1, positions),
        space=pl.ANY,
        limit=60 * 2**20,
    )
    arrived = exchange(packed, "seq", BLOCKS, IN_ROWS, np.roll(numbers, BLOCKS // 2).tolist())
    held = groups * branches * piece
    own, pair, across = call(
        table_kernel,
        [shape((held, LANES)), shape((2 * held, LANES)), shape((held, LANES))],
        [pltpu.VMEM((reds * 16, width_rows), F32), pltpu.VMEM((reds * 16, vocabulary), F32)],
        proj_weight.transpose(1, 2, 3, 0),
        embedding,
    )
    pair = lax.ppermute(pair, "red", [(q, q ^ 1) for q in range(reds)])
    across = lax.ppermute(across + pair[held:], "red", [(q, q ^ 2) for q in range(reds)])
    parts = [own, pair, across]
    constants = [jnp.asarray(c) for c in transform_constants()]
    results, grads = call(
        functools.partial(conv_kernel, scale),
        [shape((BLOCKS * OUT_ROWS, LANES)), shape((BLOCKS * 16, LANES))],
        [],
        arrived,
        *parts,
        *constants,
    )
    returned = exchange(results, "seq", BLOCKS, OUT_ROWS, numbers.reshape(-1, PLANE)[::-1].ravel().tolist())
    sums = call(
        sums_kernel,
        shape((groups * 16, LANES)),
        [pltpu.VMEM((BLOCKS, LANES), jnp.int32)],
        arrived,
        grads,
    )
    gathered = lax.all_gather(sums, "red", axis=0)
    weight_grad = call(
        functools.partial(weight_kernel, scale),
        shape((branches, reds, piece, width_rows)),
        [],
        gathered,
        embedding,
    )
    output, filter_grad, branch_grads = call(
        unpack_kernel,
        [
            shape((positions, channels)),
            shape((positions, channels)),
            shape((branches, positions, channels), BF16),
        ],
        [pltpu.VMEM((OUT_ROWS // OWN, channels, LANES), F32)],
        returned,
    )
    return output, filter_grad, branch_grads.transpose(1, 0, 2), weight_grad.transpose(3, 0, 1, 2)


def solution(mesh):
    in_specs = (
        P("seq"),
        P(None, "red"),
        P("red", None, None, "seq"),
        P("seq", "red"),
        P("seq", "red"),
    )
    out_specs = (
        P("seq", "red"),
        P("seq", "red"),
        P("seq", None, "red"),
        P("red", None, None, "seq"),
    )
    return jax.shard_map(shards, mesh=mesh, in_specs=in_specs, out_specs=out_specs, check_vma=False)
```
